256 devices in a mesh: section: 2 (over core), rep: 8 (over y, x_lo), fsdp: 16 (over x_hi, z).
Axes of the slice: x: 4 (x_hi: 2, x_lo: 2; x = x_hi * 2 + x_lo), y: 4, z: 8, core: 2. Of those that a mesh axis runs over, the one named last changes fastest.
Arguments:
- layer_input: bfloat16 [2, 2, 8192, 8192], P('section', None, ('rep', 'fsdp')), may hold values from -600 to 600
- value_grad: bfloat16 [2, 2, 8192, 1024], P('section', None, ('rep', 'fsdp')), may hold values from -7 to 7
- value_weight: bfloat16 [2, 8192, 1024], P('section', 'fsdp'), may hold values from -2 to 2
- norm_gain: bfloat16 [2, 8192], P('section', 'fsdp'), may hold values from 0.25 to 1.75
- top_grad: bfloat16 [2, 8192, 8192], P(None, ('rep', 'fsdp')), may hold values from -6 to 6
Outputs:
- input_grad: bfloat16 [2, 2, 8192, 8192], P('section', None, ('rep', 'fsdp'))
- weight_grad: float32 [2, 8192, 1024], P('section', 'fsdp')
- gain_grad: float32 [2, 8192], P('section', 'fsdp')
The draws below stay inside these ranges and needn't reach their ends.
All inputs are finite; a program needn't handle non-finite values.
Results may differ from the reference program's by a relative error of at most 0.0041.
Values may be sent and summed in bfloat16 or wider, within the bound.
A program may use at most 128 MiB of HBM per device.

```python
import math
import jax
import jax.numpy as jnp
from jax import lax

MODEL_WIDTH = 8192
MICRO = 2
TOK_DEV = 64
VW = 1024
TOKENS = 8192
N_SECTION = 2


def shared_terms(key):
    grad_key = jax.random.fold_in(key, 101)
    sign_key = jax.random.fold_in(key, 102)
    grad_base = jnp.clip(jax.random.normal(grad_key, (N_SECTION, MICRO, TOKENS, VW), jnp.float32), -3.0, 3.0)
    feature_sign = 2.0 * jax.random.randint(sign_key, (N_SECTION, MODEL_WIDTH), 0, 2).astype(jnp.float32) - 1.0
    return (grad_base, feature_sign)


def draw_layer_input(key, part):
    grad_base, feature_sign = shared_terms(key)
    key = jax.random.fold_in(key, 1)
    jitter_key, token_key, row_key, column_key, pair_key = jax.random.split(key, 5)
    array_shape = (N_SECTION, MICRO, TOKENS, MODEL_WIDTH)
    jitter = jnp.clip(jax.random.normal(jitter_key, array_shape, jnp.float32), -3.0, 3.0)
    ramp_slope = 0.6
    token_sign = 2.0 * jax.random.randint(token_key, (N_SECTION, MICRO, TOKENS, 1), 0, 2).astype(jnp.float32) - 1.0
    row_scale = jnp.exp(jax.random.uniform(row_key, (N_SECTION, MICRO, TOKENS, 1), jnp.float32, 0.0, math.log(10.0)))
    feature = jnp.arange(MODEL_WIDTH)
    ramp_term = ramp_slope * (2.0 * feature.astype(jnp.float32) / (MODEL_WIDTH - 1) - 1.0)
    column_scale = jnp.exp(jax.random.uniform(column_key, (N_SECTION, 1, 1, MODEL_WIDTH), jnp.float32, -math.log(2.0), math.log(2.0)) + ramp_term)
    blocks = TOKENS // TOK_DEV
    pairing = jax.random.permutation(pair_key, blocks)
    token_block = jnp.arange(TOKENS) // TOK_DEV
    feature_block = feature * blocks // MODEL_WIDTH
    spike_gain = jnp.where(pairing[token_block][:, None] == feature_block[None, :], 2.0, 1.0)
    tiled_grad = jnp.take(grad_base, feature % VW, axis=3)
    value_entries = row_scale * column_scale * spike_gain * (jitter + token_sign * feature_sign[:, None, None, :] * tiled_grad)
    return value_entries.astype(jnp.bfloat16)


def draw_value_grad(key, part):
    grad_base, feature_sign = shared_terms(key)
    value_entries = 1.5 * grad_base
    return value_entries.astype(jnp.bfloat16)


def draw_value_weight(key, part):
    grad_base, feature_sign = shared_terms(key)
    key = jax.random.fold_in(key, 3)
    weight_shape = (N_SECTION, MODEL_WIDTH, VW)
    random_part = jnp.clip(jax.random.normal(key, weight_shape, jnp.float32), -3.0, 3.0)
    matched = (jnp.arange(MODEL_WIDTH)[:, None] % VW == jnp.arange(VW)[None, :]).astype(jnp.float32)
    value_entries = random_part * MODEL_WIDTH ** (-0.5) + feature_sign[:, :, None] * matched * math.sqrt(VW / MODEL_WIDTH)
    return value_entries.astype(jnp.bfloat16)


def block_levels(own_key, dims, cuts, least, high):
    level, own = 1.0, jax.random.fold_in(own_key, 6)
    for position, blocks in cuts:
        steps = jnp.exp(jax.random.uniform(jax.random.fold_in(own, position), (blocks,), jnp.float32, least / len(cuts), high / len(cuts)))
        level = level * jnp.repeat(steps, dims[position] // blocks).reshape([-1 if axis == position else 1 for axis in range(len(dims))])
    return level


def normal_values(rng, shape, deviation, bound, pieces=(), dtype=jnp.bfloat16):
    result = jax.random.normal(rng, shape, jnp.float32) * deviation
    if len(pieces) > 0:
        result = block_levels(rng, shape, pieces, -0.22, 0.18) * result
    return jnp.clip(result, min=-bound, max=bound).astype(dtype)


def setup_inputs(seed: int = 0) -> dict:
    splits = jax.random.split(jax.random.key(seed), 6)
    return {
        "layer_input": draw_layer_input(jax.random.fold_in(splits[5], 71), 0),
        "value_grad": draw_value_grad(jax.random.fold_in(splits[5], 71), 0),
        "value_weight": draw_value_weight(jax.random.fold_in(splits[5], 71), 0),
        "norm_gain": jnp.clip(1.0 + 0.15 * jax.random.normal(splits[3], (N_SECTION, MODEL_WIDTH), jnp.float32), 0.25, 1.75).astype(jnp.bfloat16),
        "top_grad": normal_values(splits[4], (MICRO, TOKENS, MODEL_WIDTH), 1.0, 6.0, ((1, 128),)),
    }


norm_eps = 1e-05

def section_terms(inputs, grads, weight, gain):
    value_entries = inputs.astype(jnp.float32)
    inverse_scale = jax.lax.rsqrt(lax.optimization_barrier(jnp.mean(value_entries * value_entries, axis=1)) + norm_eps)
    centered_input = value_entries * inverse_scale[:, None]
    gain_float_full = gain.astype(jnp.float32)
    normalized_input = (centered_input * gain_float_full).astype(jnp.bfloat16)
    weight_part = jnp.dot(normalized_input.T, grads, preferred_element_type=jnp.float32)
    normalized_gradient = jnp.dot(grads, weight.T, preferred_element_type=jnp.float32)
    gain_portion = lax.optimization_barrier(jnp.sum(normalized_gradient * centered_input, axis=0))
    centered_gradient = normalized_gradient * gain_float_full
    average_product = lax.optimization_barrier(jnp.sum(centered_gradient * centered_input, axis=1)) / MODEL_WIDTH
    local_piece = (inverse_scale[:, None] * (centered_gradient - centered_input * average_product[:, None])).astype(jnp.bfloat16)
    return (weight_part, gain_portion, local_piece)

def reference(layer_input, value_grad, value_weight, norm_gain, top_grad):
    norm_scale = float(MICRO * TOKENS) ** (-0.5)
    upper_list = []
    lower_list = []
    weight_grads = [None, None]
    gain_grads = [None, None]
    for section_id in (1, 0):
        weight_total = jnp.zeros((MODEL_WIDTH, VW), jnp.float32)
        gain_total = jnp.zeros((MODEL_WIDTH,), jnp.float32)
        for batch_index in range(MICRO):
            weight_part, gain_portion, local_piece = section_terms(layer_input[section_id, batch_index], value_grad[section_id, batch_index], value_weight[section_id], norm_gain[section_id])
            weight_total = weight_total + weight_part
            gain_total = gain_total + gain_portion
            if section_id == 1:
                upper_list.append((top_grad[batch_index].astype(jnp.float32) + local_piece.astype(jnp.float32)).astype(jnp.bfloat16))
            else:
                lower_list.append((upper_list[batch_index].astype(jnp.float32) + local_piece.astype(jnp.float32)).astype(jnp.bfloat16))
        weight_grads[section_id] = weight_total * norm_scale
        gain_grads[section_id] = gain_total * norm_scale
    input_grad = jnp.stack([jnp.stack(lower_list), jnp.stack(upper_list)])
    return (input_grad, jnp.stack(weight_grads), jnp.stack(gain_grads))
```

```python
import functools

import jax
import jax.numpy as jnp
from jax import lax
from jax.experimental import pallas as pl
from jax.experimental.pallas import tpu as pltpu
from jax.sharding import PartitionSpec as P

NORM_EPS = 1e-05
MESH = pl.DeviceIdType.MESH
NZ = 8
NY = 4
F32 = jnp.float32
BF16 = jnp.bfloat16


def remote(src, dst, send_sem, recv_sem, device):
    return pltpu.make_async_remote_copy(
        src_ref=src, dst_ref=dst, send_sem=send_sem, recv_sem=recv_sem, device_id=device, device_id_type=MESH
    )


def kernel(
    norm_scale,
    x_hbm, g_hbm, w_hbm, gain_ref, top_hbm,
    ig_ref, wg_ref, gg_ref,
    xbuf, topbuf, wown, gain_src, gain_all, scale_buf, nb, xr, gr, wr, pb, ra, sb, rb, ag, db, dr, upper, ggbuf,
    local_sem, gain_ss, gain_rs, g_ss, g_rs, x_ss, x_rs, w_ss, w_rs, w2_ss, w2_rs,
    a_ss, a_rs, b_ss, b_rs, c_ss, c_rs, q_ss, q_rs, d_ss, d_rs, u_ss, u_rs,
):
    tokens, width = xbuf.shape
    half = tokens // 2
    blocks, _, bw = nb.shape
    vw = gr.shape[1]
    rows = sb.shape[1]
    rep = lax.axis_index("rep")
    fs = lax.axis_index("fsdp")
    sec = lax.axis_index("section")
    xl, y, xh, z = rep % 2, rep // 2, fs // NZ, fs % NZ
    yp = (y + 1 + 2 * ((y + sec) % 2)) % NY
    zp = (z + 1 + (NZ - 2) * ((z + sec) % 2)) % NZ
    jy, jz = y % 2, z % 2
    me = xh * 4 + jy * 2 + jz

    def zprime(ky, kz, i):
        return kz + 2 * ((2 * ky + i + 2 * sec) % 4)

    def member(flip):
        fh, fy, fz = flip // 4, (flip // 2) % 2, flip % 2
        mxl = xl + fh * (1 - 2 * xl)
        mxh = xh + fh * (1 - 2 * xh)
        my = y + fy * (yp - y)
        mz = z + fz * (zp - z)
        label = (mxh, my % 2, mz % 2)
        device = {"rep": my * 2 + mxl, "fsdp": mxh * NZ + mz}
        return device, label, label[0] * 4 + label[1] * 2 + label[2]

    def block(label, i):
        return label[0] * NZ + zprime(label[1], label[2], i)

    xcopy = pltpu.make_async_copy(x_hbm, xbuf, local_sem.at[0])
    xcopy.start()
    tcopy = pltpu.make_async_copy(top_hbm, topbuf, local_sem.at[1])
    tcopy.start()
    wcopy = pltpu.make_async_copy(w_hbm, wown, local_sem.at[2])
    wcopy.start()
    my_rows = pl.ds(pl.multiple_of(me * tokens, tokens), tokens)
    gcopy = pltpu.make_async_copy(g_hbm, gr.at[my_rows], local_sem.at[3])
    gcopy.start()
    gain_f = jnp.broadcast_to(gain_ref[...].astype(F32), gain_src.shape)
    gain_src[...] = gain_f
    gain_all[fs] = gain_f

    barrier = pltpu.get_barrier_semaphore()

    def hello(device):
        pl.semaphore_signal(barrier, inc=1, device_id=device, device_id_type=MESH)

    @pl.loop(1, 8)
    def _(f):
        hello(member(f)[0])
        hello({"rep": (rep + f) % 8})

    @pl.loop(1, 16)
    def _(k):
        hello({"fsdp": (fs + k) % 16})

    hello({"section": 1 - sec})
    pl.semaphore_wait(barrier, 7 + 7 + 15 + 1)

    @pl.loop(1, 16)
    def _(k):
        remote(gain_src, gain_all.at[fs], gain_ss.at[k], gain_rs.at[fs], {"fsdp": (fs + k) % 16}).start()

    def g_copy(n, f, owner, src):
        dst = gr.at[pl.ds(pl.multiple_of(owner * tokens, tokens), tokens)]
        return remote(src, dst, g_ss.at[n], g_rs.at[owner], member(f)[0])

    for n, f in enumerate((4, 1, 2, 3)):
        g_copy(n, f, me, g_hbm).start()

    root = z == zprime(jy, jz, xl)
    wh = w_hbm.shape[0] // 2
    w_parts = [pl.ds(0, wh), pl.ds(wh, wh)]

    def w_copy(n, p):
        return remote(
            w_hbm.at[w_parts[p]], wr.at[xl, w_parts[p]], w_ss.at[n, p], w_rs.at[p],
            {"fsdp": xh * NZ + (z + (2, 6, 4)[n]) % NZ},
        )

    def w_local(p):
        return pltpu.make_async_copy(w_hbm.at[w_parts[p]], wr.at[xl, w_parts[p]], local_sem.at[4 + p])

    @pl.when(root)
    def _():
        for p in range(2):
            w_local(p).start()
            for n in range(3):
                w_copy(n, p).start()

    xcopy.wait()

    def columns(b):
        return pl.ds(pl.multiple_of(b * bw, bw), bw)

    def squares(b, acc):
        v = xbuf[:, columns(b)].astype(F32)
        v = v * v
        for k in range(bw // 128):
            acc = acc + v[:, k * 128 : (k + 1) * 128]
        return acc

    acc = lax.fori_loop(0, blocks, squares, jnp.zeros((tokens, 128), F32))
    scale = lax.rsqrt(jnp.sum(acc, axis=1, keepdims=True) / width + NORM_EPS)
    scale_buf[...] = jnp.broadcast_to(scale, scale_buf.shape)

    @pl.loop(1, 16)
    def _(k):
        src = (fs + k) % 16
        remote(gain_src, gain_all.at[src], gain_ss.at[k], gain_rs.at[src], {"fsdp": src}).wait_recv()

    @pl.loop(0, blocks)
    def _(b):
        v = xbuf[:, columns(b)].astype(F32) * scale_buf[:, 0:1]
        nb[b] = (v * gain_all[b, 0:1, :]).astype(BF16)

    def x_copy(f, i):
        device, label, _ = member(f)
        return remote(nb.at[block(label, i)], xr.at[i, my_rows], x_ss.at[f, i], x_rs.at[me, i], device)

    for i in range(2):
        @pl.loop(1, 8)
        def _(f):
            x_copy(f, i).start()

    for i in range(2):
        xr[i, my_rows] = nb[block((xh, jy, jz), i)]

    other = (me + 4) % 8
    other_rows = pl.ds(pl.multiple_of(other * tokens, tokens), tokens)
    g_copy(0, 4, other, g_hbm).wait_recv()
    for n, f in enumerate((1, 2, 3)):
        g_copy(4 + n, f, other, gr.at[other_rows]).start()

    gcopy.wait()

    @pl.loop(1, 8)
    def _(f):
        m = member(f)[2]

        @pl.when(f != 4)
        def _():
            g_copy(0, 4, m, g_hbm).wait_recv()

    def wgrad(i):
        @pl.loop(1, 8)
        def _(f):
            m = member(f)[2]
            dst = xr.at[i, pl.ds(pl.multiple_of(m * tokens, tokens), tokens)]
            remote(nb.at[0], dst, x_ss.at[f, i], x_rs.at[m, i], {"section": sec}).wait_recv()

        part = lax.dot_general(xr[i], gr[...], (((0,), (0,)), ((), ())), preferred_element_type=F32)
        pb[i] = part.astype(BF16)

        @pl.loop(1, 8)
        def _(k):
            c = (rep + k) % 8
            a_copy(k, i, c).start()

        ra[rep, i] = pb[i, pl.ds(pl.multiple_of(rep * rows, rows), rows)]

    def a_copy(k, i, c):
        return remote(
            pb.at[i, pl.ds(pl.multiple_of(c * rows, rows), rows)], ra.at[rep, i],
            a_ss.at[k, i], a_rs.at[rep, i], {"rep": c},
        )

    for i in range(2):
        wgrad(i)

    def w_swap(p):
        return remote(
            wr.at[xl, w_parts[p]], wr.at[xl, w_parts[p]], w2_ss.at[p], w2_rs.at[p], {"rep": y * 2 + 1 - xl}
        )

    for p in range(2):
        @pl.when(root)
        def _():
            w_local(p).wait()

        @pl.when(jnp.logical_not(root))
        def _():
            w_copy(0, p).wait_recv()

        w_swap(p).start()

    @pl.loop(1, 8)
    def _(k):
        c = (rep + k) % 8
        for i in range(2):
            remote(pb.at[i, pl.ds(0, rows)], ra.at[c, i], a_ss.at[k, i], a_rs.at[c, i], {"rep": c}).wait_recv()

    for ky in range(2):
        for i in range(2):
            total = ra[2 * ky, i].astype(F32) + ra[2 * ky + 1, i].astype(F32)
            total = total + (ra[2 * ky + 4, i].astype(F32) + ra[2 * ky + 5, i].astype(F32))
            sb[2 * ky + i] = total.astype(BF16)

    zk = z // 2

    def b_copy(k):
        slot = (zk + k) % 4
        return remote(
            sb.at[(slot + 2 * sec) % 4], rb.at[zk], b_ss.at[k], b_rs.at[zk], {"fsdp": xh * NZ + jz + 2 * slot}
        )

    for k in range(1, 4):
        b_copy(k).start()
    rb[zk] = sb[(zk + 2 * sec) % 4]

    for p in range(2):
        remote(
            wr.at[1 - xl, w_parts[p]], wr.at[1 - xl, w_parts[p]], w2_ss.at[p], w2_rs.at[p], {"section": sec}
        ).wait_recv()

    def d_copy(f, i):
        device, _, m = member(f)
        return remote(
            db.at[i, pl.ds(pl.multiple_of(m * tokens, tokens), tokens)], dr.at[block((xh, jy, jz), i)],
            d_ss.at[f, i], d_rs.at[block((xh, jy, jz), i)], device,
        )

    for i in range(2):
        back = lax.dot_general(gr[...], wr[i], (((1,), (1,)), ((), ())), preferred_element_type=F32)
        db[i] = back.astype(BF16)

        @pl.loop(1, 8)
        def _(f):
            d_copy(f, i).start()

        dr[block((xh, jy, jz), i)] = db[i, my_rows]

    for k in range(1, 4):
        slot = (zk + k) % 4
        remote(sb.at[0], rb.at[slot], b_ss.at[k], b_rs.at[slot], {"section": sec}).wait_recv()
    total = (rb[0].astype(F32) + rb[1].astype(F32)) + (rb[2].astype(F32) + rb[3].astype(F32))
    total = total * norm_scale
    ag[rep] = total.astype(BF16)
    wcopy.wait()
    gg = jnp.sum(total * wown[pl.ds(pl.multiple_of(rep * rows, rows), rows)].astype(F32), axis=1, keepdims=True)
    gg = jnp.broadcast_to(jnp.concatenate([gg, gg], axis=0), (2 * rows, 128))
    ggbuf[rep] = gg.T[0:8]

    def c_copy(k, c):
        return remote(ag.at[rep], ag.at[rep], c_ss.at[k], c_rs.at[rep], {"rep": c})

    def q_copy(k, c):
        return remote(ggbuf.at[rep], ggbuf.at[rep], q_ss.at[k], q_rs.at[rep], {"rep": c})

    @pl.loop(1, 8)
    def _(k):
        c_copy(k, (rep + k) % 8).start()
        q_copy(k, (rep + k) % 8).start()

    tcopy.wait()

    @pl.loop(1, 8)
    def _(f):
        label = member(f)[1]
        for i in range(2):
            b = block(label, i)
            remote(db.at[0, pl.ds(0, tokens)], dr.at[b], d_ss.at[f, i], d_rs.at[b], {"section": sec}).wait_recv()

    def u_copy(mi):
        part = pl.ds(mi * half, half)
        return remote(ig_ref.at[part], upper.at[part], u_ss.at[mi], u_rs.at[mi], {"section": 0})

    for mi in range(2):
        part = pl.ds(mi * half, half)

        def dots(b, acc):
            v = dr[b, part].astype(F32) * gain_all[b, 0:1, :]
            v = v * (xbuf[part, columns(b)].astype(F32) * scale_buf[part, 0:1])
            for k in range(bw // 128):
                acc = acc + v[:, k * 128 : (k + 1) * 128]
            return acc

        acc = lax.fori_loop(0, blocks, dots, jnp.zeros((half, 128), F32))
        avg = jnp.sum(acc, axis=1, keepdims=True) / width

        def finish(addend):
            @pl.loop(0, blocks)
            def _(b):
                sc = scale_buf[part, 0:1]
                v = dr[b, part].astype(F32) * gain_all[b, 0:1, :]
                v = sc * (v - xbuf[part, columns(b)].astype(F32) * sc * avg)
                v = v.astype(BF16).astype(F32)
                ig_ref[part, columns(b)] = (addend[part, columns(b)].astype(F32) + v).astype(BF16)

        @pl.when(sec == 1)
        def _():
            finish(topbuf)
            u_copy(mi).start()

        @pl.when(sec == 0)
        def _():
            u_copy(mi).wait_recv()
            finish(upper)

    @pl.loop(1, 8)
    def _(k):
        c = (rep + k) % 8
        remote(ag.at[c], ag.at[c], c_ss.at[k], c_rs.at[c], {"rep": c}).wait_recv()
        remote(ggbuf.at[c], ggbuf.at[c], q_ss.at[k], q_rs.at[c], {"rep": c}).wait_recv()

    for c in range(8):
        wg_ref[c * rows : (c + 1) * rows] = ag[c].astype(F32)
        gg_ref[c : c + 1] = ggbuf[c, 0:1]

    @pl.loop(1, 16)
    def _(k):
        remote(gain_src, gain_all.at[fs], gain_ss.at[k], gain_rs.at[fs], {"fsdp": (fs + k) % 16}).wait_send()

    for n, f in enumerate((4, 1, 2, 3)):
        g_copy(n, f, me, g_hbm).wait_send()
    for n, f in enumerate((1, 2, 3)):
        g_copy(4 + n, f, other, gr.at[other_rows]).wait_send()

    @pl.when(root)
    def _():
        for p in range(2):
            for n in range(3):
                w_copy(n, p).wait_send()

    for p in range(2):
        w_swap(p).wait_send()

    @pl.loop(1, 8)
    def _(k):
        c = (rep + k) % 8
        for i in range(2):
            x_copy(k, i).wait_send()
            a_copy(k, i, c).wait_send()
            d_copy(k, i).wait_send()
        c_copy(k, c).wait_send()
        q_copy(k, c).wait_send()

    for k in range(1, 4):
        b_copy(k).wait_send()

    @pl.when(sec == 1)
    def _():
        for mi in range(2):
            u_copy(mi).wait_send()


def local(layer_input, value_grad, value_weight, norm_gain, top_grad):
    reps, groups = lax.axis_size("rep"), lax.axis_size("fsdp")
    _, micro, rows, width = layer_input.shape
    vw = value_grad.shape[3]
    tokens = micro * rows
    bw = value_weight.shape[1]
    blocks = width // bw
    slice_rows = bw // reps
    norm_scale = float(tokens * reps * groups) ** (-0.5)
    any_spec = pl.BlockSpec(memory_space=pl.ANY)
    vmem = pl.BlockSpec(memory_space=pltpu.VMEM)
    dma = pltpu.SemaphoreType.DMA
    grad, wgrad, ggrad = pl.pallas_call(
        functools.partial(kernel, norm_scale),
        out_shape=(
            jax.ShapeDtypeStruct((tokens, width), BF16),
            jax.ShapeDtypeStruct((bw, vw), F32),
            jax.ShapeDtypeStruct((8, 128), F32),
        ),
        in_specs=[any_spec, any_spec, any_spec, vmem, any_spec],
        out_specs=(vmem, vmem, vmem),
        scratch_shapes=[
            pltpu.VMEM((tokens, width), BF16),
            pltpu.VMEM((tokens, width), BF16),
            pltpu.VMEM((bw, vw), BF16),
            pltpu.VMEM((8, bw), F32),
            pltpu.VMEM((blocks, 8, bw), F32),
            pltpu.VMEM((tokens, 128), F32),
            pltpu.VMEM((blocks, tokens, bw), BF16),
            pltpu.VMEM((2, 8 * tokens, bw), BF16),
            pltpu.VMEM((8 * tokens, vw), BF16),
            pltpu.VMEM((2, bw, vw), BF16),
            pltpu.VMEM((2, bw, vw), BF16),
            pltpu.VMEM((8, 2, slice_rows, vw), BF16),
            pltpu.VMEM((4, slice_rows, vw), BF16),
            pltpu.VMEM((4, slice_rows, vw), BF16),
            pltpu.VMEM((8, slice_rows, vw), BF16),
            pltpu.VMEM((2, 8 * tokens, bw), BF16),
            pltpu.VMEM((blocks, tokens, bw), BF16),
            pltpu.VMEM((tokens, width), BF16),
            pltpu.VMEM((8, 8, 128), F32),
            dma((6,)),
            dma((16,)), dma((16,)),
            dma((7,)), dma((8,)),
            dma((8, 2)), dma((8, 2)),
            dma((3, 2)), dma((2,)), dma((2,)), dma((2,)),
            dma((8, 2)), dma((8, 2)),
            dma((4,)), dma((4,)),
            dma((8,)), dma((8,)), dma((8,)), dma((8,)),
            dma((8, 2)), dma((16,)),
            dma((2,)), dma((2,)),
        ],
        compiler_params=pltpu.CompilerParams(
            collective_id=0, has_side_effects=True, vmem_limit_bytes=60 * 1024 * 1024
        ),
        name="relay",
    )(
        layer_input.reshape(tokens, width),
        value_grad.reshape(tokens, vw),
        value_weight[0],
        norm_gain,
        top_grad.reshape(tokens, width),
    )
    gain_grad = ggrad[:, :slice_rows].reshape(1, bw) / norm_gain.astype(F32)
    return grad.reshape(layer_input.shape), wgrad[None], gain_grad


def solution(mesh):
    return jax.shard_map(
        local,
        mesh=mesh,
        in_specs=(
            P("section", None, ("rep", "fsdp"), None),
            P("section", None, ("rep", "fsdp"), None),
            P("section", "fsdp", None),
            P("section", "fsdp"),
            P(None, ("rep", "fsdp"), None),
        ),
        out_specs=(
            P("section", None, ("rep", "fsdp"), None),
            P("section", "fsdp", None),
            P("section", "fsdp"),
        ),
        check_vma=False,
    )
```

```python
import functools

import jax
import jax.numpy as jnp
from jax import lax
from jax.experimental import pallas as pl
from jax.experimental.pallas import tpu as pltpu
from jax.sharding import PartitionSpec as P

NORM_EPS = 1e-05
MESH = pl.DeviceIdType.MESH
NZ = 8
NY = 4
F32 = jnp.float32
BF16 = jnp.bfloat16


def remote(src, dst, send_sem, recv_sem, device):
    return pltpu.make_async_remote_copy(
        src_ref=src, dst_ref=dst, send_sem=send_sem, recv_sem=recv_sem, device_id=device, device_id_type=MESH
    )


def kernel(
    norm_scale,
    x_hbm, g_hbm, w_hbm, gain_ref, top_hbm,
    ig_ref, wg_ref, gg_ref,
    xbuf, topbuf, wown, gain_src, gain_all, scale_buf, gx, acc_buf, nb, xr, gr, wr, pt, rt, po, pb, ra, sb, rb, db, dr, upper, ggbuf,
    local_sem, gain_ss, gain_rs, g_ss, g_rs, x_ss, x_rs, w_ss, w_rs, w2_ss, w2_rs, w3_ss, w3_rs,
    t_ss, t_rs,     a_ss, a_rs, b_ss, b_rs, c_ss, c_rs, q_ss, q_rs, d_ss, d_rs, u_ss, u_rs,
):
    tokens, width = xbuf.shape
    blocks, _, bw = gain_all.shape
    hw = bw // 2
    vw = gr.shape[1]
    rows = sb.shape[2]
    rep = lax.axis_index("rep")
    fs = lax.axis_index("fsdp")
    sec = lax.axis_index("section")
    xl, y, xh, z = rep % 2, rep // 2, fs // NZ, fs % NZ
    yp = (y + 1 + 2 * ((y + sec) % 2)) % NY
    zp = (z + 1 + (NZ - 2) * ((z + sec) % 2)) % NZ
    jy, jz = y % 2, z % 2
    xb = xh + sec * ((xl + xh) % 2 - xh)
    side = xl + sec * (xh - xl)
    twin = {"rep": y * 2 + 1 - xl, "fsdp": (xh + sec * (1 - 2 * xh)) * NZ + z}
    me = xb * 4 + jy * 2 + jz

    def half_of(label, i):
        return label[0] + sec * (i - label[0])

    def zprime(label, i):
        return label[2] + 2 * ((2 * label[1] + i + sec * ((label[0] + i) % 2 - i + 2)) % 4)

    def member(flip):
        fh, fy, fz = flip // 4, (flip // 2) % 2, flip % 2
        mxl = xl + fh * (1 - 2 * xl)
        mxh = xh + fh * (1 - sec) * (1 - 2 * xh)
        my = y + fy * (yp - y)
        mz = z + fz * (zp - z)
        label = (xb + fh * (1 - 2 * xb), my % 2, mz % 2)
        device = {"rep": my * 2 + mxl, "fsdp": mxh * NZ + mz}
        return device, label, label[0] * 4 + label[1] * 2 + label[2]

    def block(label, i):
        return half_of(label, i) * NZ + zprime(label, i)

    mine = (xb, jy, jz)

    def rows_of(m):
        return pl.ds(pl.multiple_of(m * tokens, tokens), tokens)

    my_rows = rows_of(me)
    other = (me + 4) % 8

    def columns(b):
        return pl.ds(pl.multiple_of(b * bw, bw), bw)

    xcopy = pltpu.make_async_copy(x_hbm, xbuf, local_sem.at[0])
    tcopy = pltpu.make_async_copy(top_hbm, topbuf, local_sem.at[1])
    wcopy = pltpu.make_async_copy(w_hbm, wown, local_sem.at[2])
    gcopy = pltpu.make_async_copy(g_hbm, gr.at[my_rows], local_sem.at[3])

    def local_start():
        for copy in (xcopy, gcopy, wcopy, tcopy):
            copy.start()
        gain_f = jnp.broadcast_to(gain_ref[...].astype(F32), gain_src.shape)
        gain_src[...] = gain_f
        gain_all[fs] = gain_f

    def meet():
        barrier = pltpu.get_barrier_semaphore()

        def hello(device):
            pl.semaphore_signal(barrier, inc=1, device_id=device, device_id_type=MESH)

        @pl.loop(1, 8)
        def _(f):
            hello(member(f)[0])
            hello({"rep": (rep + f) % 8})
            hello({"rep": (rep + f) % 8, "fsdp": (1 - xh) * NZ + z})

        @pl.loop(1, 16)
        def _(k):
            hello({"fsdp": (fs + k) % 16})

        hello({"section": 1 - sec})
        pl.semaphore_wait(barrier, 3 * 7 + 15 + 1)

    def gain_copy(k, owner):
        return remote(gain_src, gain_all.at[owner], gain_ss.at[k], gain_rs.at[owner], {"fsdp": (fs + k) % 16})

    def gains_start():
        @pl.loop(1, 16)
        def _(k):
            gain_copy(k, fs).start()

    def gains_wait():
        @pl.loop(1, 16)
        def _(k):
            gain_copy(k, (fs + k) % 16).wait_recv()

    def g_copy(n, f, owner, src):
        return remote(src, gr.at[rows_of(owner)], g_ss.at[n], g_rs.at[owner], member(f)[0])

    def grads_start():
        for n, f in enumerate((4, 1, 2, 3)):
            g_copy(n, f, me, g_hbm).start()

    def grads_pass():
        g_copy(0, 4, other, g_hbm).wait_recv()
        for n, f in enumerate((1, 2, 3)):
            g_copy(4 + n, f, other, gr.at[rows_of(other)]).start()

    def grads_wait():
        gcopy.wait()

        @pl.loop(1, 8)
        def _(f):
            @pl.when(f != 4)
            def _():
                g_copy(0, 4, member(f)[2], g_hbm).wait_recv()

    root = z == zprime(mine, side)
    wh = w_hbm.shape[0] // 2
    yh = y // 2

    def w_part(p):
        return pl.ds(pl.multiple_of(p * wh, wh), wh)

    def w_copy(n):
        return remote(
            w_hbm.at[w_part(yh)], wr.at[side, w_part(yh)], w_ss.at[n], w_rs.at[0],
            {"fsdp": xh * NZ + (z + (2, 6, 4)[n]) % NZ},
        )

    w_local = pltpu.make_async_copy(w_hbm.at[w_part(yh)], wr.at[side, w_part(yh)], local_sem.at[4])

    def w_across(p):
        return remote(
            wr.at[side, w_part(yh)], wr.at[side, w_part(p)], w2_ss.at[0], w2_rs.at[0], {"rep": ((y + 2) % NY) * 2 + xl}
        )

    def w_swap(n, p, owner):
        return remote(
            wr.at[side, w_part(p)], wr.at[owner, w_part(p)], w3_ss.at[n], w3_rs.at[p], twin
        )

    def weights_start():
        @pl.when(root)
        def _():
            w_local.start()
            for n in range(3):
                w_copy(n).start()

    def weights_across():
        @pl.when(root)
        def _():
            w_local.wait()

        @pl.when(jnp.logical_not(root))
        def _():
            w_copy(0).wait_recv()

        w_across(yh).start()
        w_swap(0, yh, side).start()

    def weights_pass():
        w_across(1 - yh).wait_recv()
        w_swap(1, 1 - yh, side).start()

    def swap_wait(p):
        w_swap(0, p, 1 - side).wait_recv()

    def scales():
        xcopy.wait()

        def squares(b, acc):
            v = xbuf[:, columns(b)].astype(F32)
            v = v * v
            for k in range(bw // 128):
                acc = acc + v[:, k * 128 : (k + 1) * 128]
            return acc

        acc = lax.fori_loop(0, blocks, squares, jnp.zeros((tokens, 128), F32))
        scale = lax.rsqrt(jnp.sum(acc, axis=1, keepdims=True) / width + NORM_EPS)
        scale_buf[...] = jnp.broadcast_to(scale, scale_buf.shape)

    def norm():
        @pl.loop(0, blocks)
        def _(b):
            v = xbuf[:, columns(b)].astype(F32) * scale_buf[:, 0:1]
            v = v * gain_all[b, 0:1, :]
            for h in range(2):
                gx[b, h] = v[:, h * hw : (h + 1) * hw]
                nb[b, h] = v[:, h * hw : (h + 1) * hw].astype(BF16)

    def x_copy(f, n, owner):
        device, label, _ = member(f)
        return remote(
            nb.at[block(label, n % 2), n // 2], xr.at[n, rows_of(owner)], x_ss.at[f, n], x_rs.at[owner, n], device
        )

    def normed_start(h):
        for i in range(2):
            n = 2 * h + i

            @pl.loop(1, 8)
            def _(f):
                x_copy(f, n, me).start()

            xr[n, my_rows] = nb[block(mine, i), h]

    def normed_wait(h):
        @pl.loop(1, 8)
        def _(f):
            for i in range(2):
                x_copy(f, 2 * h + i, member(f)[2]).wait_recv()

    def partial(n):
        return lax.dot_general(xr[n], gr[...], (((0,), (0,)), ((), ())), preferred_element_type=F32)

    def t_copy(h):
        return remote(pt.at[h], rt.at[h], t_ss.at[h], t_rs.at[h], twin)

    def wgrad_other(h):
        pt[h] = partial(2 * h + 1 - side).astype(BF16)
        t_copy(h).start()

    def wgrad_own(h):
        po[h] = partial(2 * h + side)

    def slice_of(c):
        return pl.ds(pl.multiple_of(c * rows, rows), rows)

    def a_copy(k, h, sender):
        c = (rep + k) % 8
        return remote(pb.at[h, slice_of(c)], ra.at[h, sender], a_ss.at[k, h], a_rs.at[sender, h], {"rep": c})

    def plane_start(h):
        t_copy(h).wait_recv()
        pb[h] = (po[h] + rt[h].astype(F32)).astype(BF16)

        @pl.loop(1, 8)
        def _(k):
            a_copy(k, h, rep).start()

        ra[h, rep] = pb[h, slice_of(rep)]

    def plane_wait(h):
        @pl.loop(1, 8)
        def _(k):
            a_copy(k, h, (rep + k) % 8).wait_recv()

    def plane_sum(h):
        for ky in range(2):
            for t in range(2):
                total = ra[h, 2 * ky + t].astype(F32) + ra[h, 2 * ky + 4 + t].astype(F32)
                sb[h, 2 * ky + t] = total.astype(BF16)

    def twin_sent():
        for h in range(2):
            t_copy(h).wait_send()

    zk = z // 2

    def b_copy(k, h, sender):
        slot = (zk + k) % 4
        return remote(
            sb.at[h, (slot + 2 * sec) % 4], rb.at[h, sender], b_ss.at[k, h], b_rs.at[sender, h],
            {"fsdp": xh * NZ + jz + 2 * slot},
        )

    def z_start(h):
        for k in range(1, 4):
            b_copy(k, h, zk).start()
        rb[h, zk] = sb[h, (zk + 2 * sec) % 4]

    def z_wait(h):
        for k in range(1, 4):
            b_copy(k, h, (zk + k) % 4).wait_recv()

    def out_rows(h, c):
        return pl.ds(pl.multiple_of(h * hw + c * rows, rows), rows)

    def z_sum(h):
        if h == 0:
            wcopy.wait()
        total = (rb[h, 0].astype(F32) + rb[h, 1].astype(F32)) + (rb[h, 2].astype(F32) + rb[h, 3].astype(F32))
        total = total * norm_scale
        wg_ref[out_rows(h, rep)] = total.astype(BF16)
        gg = jnp.sum(total * wown[out_rows(h, rep)].astype(F32), axis=1, keepdims=True)
        gg = jnp.broadcast_to(jnp.concatenate([gg] * (128 // rows), axis=0), (128, 128))
        ggbuf[h, rep] = gg.T[0:8]

    def c_copy(k, h, owner):
        part = wg_ref.at[out_rows(h, owner)]
        return remote(part, part, c_ss.at[k, h], c_rs.at[owner, h], {"rep": (rep + k) % 8})

    def q_copy(k, h, owner):
        part = ggbuf.at[h, owner]
        return remote(part, part, q_ss.at[k, h], q_rs.at[owner, h], {"rep": (rep + k) % 8})

    def gather_start(h):
        @pl.loop(1, 8)
        def _(k):
            c_copy(k, h, rep).start()
            q_copy(k, h, rep).start()

    def gather_wait(h):
        @pl.loop(1, 8)
        def _(k):
            c_copy(k, h, (rep + k) % 8).wait_recv()
            q_copy(k, h, (rep + k) % 8).wait_recv()

    def gradients_out():
        for h in range(2):
            for c in range(8):
                gg_ref[8 * h + c : 8 * h + c + 1] = ggbuf[h, c, 0:1]

    def d_copy(f, i, p, b):
        device, _, m = member(f)
        return remote(db.at[i, p, rows_of(m)], dr.at[b, p], d_ss.at[f, i, p], d_rs.at[b, p], device)

    def back_start(i, p):
        back = lax.dot_general(gr[...], wr[i, w_part(p)], (((1,), (1,)), ((), ())), preferred_element_type=F32)
        db[i, p] = back.astype(BF16)
        b = block(mine, i)

        @pl.loop(1, 8)
        def _(f):
            d_copy(f, i, p, b).start()

        dr[b, p] = db[i, p, my_rows]

    def first_half(f):
        return member(f)[0]["rep"] // 4

    def back_wait(n):
        @pl.loop(1, 8)
        def _(f):
            p = (first_half(f) + n) % 2
            for i in range(2):
                d_copy(f, i, p, block(member(f)[1], i)).wait_recv()

    def back_sent():
        @pl.loop(1, 8)
        def _(f):
            for i in range(2):
                for p in range(2):
                    d_copy(f, i, p, 0).wait_send()

    def dots(n):
        def add(f, acc):
            p = (first_half(f) + n) % 2
            for i in range(2):
                b = block(member(f)[1], i)
                v = dr[b, p].astype(F32) * gx[b, p]
                for k in range(hw // 128):
                    acc = acc + v[:, k * 128 : (k + 1) * 128]
            return acc

        start = jnp.zeros((tokens, 128), F32) if n == 0 else acc_buf[...]
        acc = lax.fori_loop(0, 8, add, start)
        if n == 0:
            acc_buf[...] = acc
        else:
            scale = scale_buf[:, 0:1]
            avg = jnp.sum(acc, axis=1, keepdims=True) / width
            acc_buf[...] = jnp.broadcast_to(scale * scale * avg, acc.shape)

    parts = u_ss.shape[0]
    part_rows = tokens // parts

    def part_of(n):
        return pl.ds(pl.multiple_of(n * part_rows, part_rows), part_rows)

    def u_copy(n):
        return remote(ig_ref.at[part_of(n)], upper.at[part_of(n)], u_ss.at[n], u_rs.at[n], {"section": 0})

    def owner():
        def finish(part, top):
            sc = scale_buf[part, :]
            c2 = acc_buf[part, :]

            @pl.loop(0, blocks)
            def _(b):
                for k in range(bw // 128):
                    lanes = slice(k * 128, (k + 1) * 128)
                    cols = pl.ds(pl.multiple_of(b * bw + k * 128, 128), 128)
                    half_lanes = slice(k * 128 % hw, k * 128 % hw + 128)
                    v = dr[b, k * 128 // hw, part, half_lanes].astype(F32) * gain_all[b, 0:1, lanes] * sc
                    v = (v - xbuf[part, cols].astype(F32) * c2).astype(BF16)
                    if top:
                        v = (topbuf[part, cols].astype(F32) + v.astype(F32)).astype(BF16)
                    ig_ref[part, cols] = v

        @pl.when(sec == 1)
        def _():
            @pl.loop(0, parts)
            def _(n):
                finish(part_of(n), True)
                u_copy(n).start()

        @pl.when(sec == 0)
        def _():
            @pl.loop(0, parts)
            def _(n):
                finish(part_of(n), False)

            @pl.loop(0, parts)
            def _(n):
                u_copy(n).wait_recv()
                part = part_of(n)
                for k in range(width // 1024):
                    cols = slice(k * 1024, (k + 1) * 1024)
                    v = upper[part, cols].astype(F32) + ig_ref[part, cols].astype(F32)
                    ig_ref[part, cols] = v.astype(BF16)

    def gains_sent():
        @pl.loop(1, 16)
        def _(k):
            gain_copy(k, fs).wait_send()

    def grads_sent():
        for n, f in enumerate((4, 1, 2, 3)):
            g_copy(n, f, me, g_hbm).wait_send()

    def passed_sent():
        for n, f in enumerate((1, 2, 3)):
            g_copy(4 + n, f, other, gr.at[rows_of(other)]).wait_send()

    def weights_sent():
        @pl.when(root)
        def _():
            for n in range(3):
                w_copy(n).wait_send()

    def across_sent():
        w_across(yh).wait_send()
        w_swap(0, yh, side).wait_send()

    def swap_sent():
        w_swap(1, 1 - yh, side).wait_send()

    def all_sent(copy, i, owner):
        @pl.loop(1, 8)
        def _(k):
            copy(k, i, owner).wait_send()

    def z_sent():
        for h in range(2):
            for k in range(1, 4):
                b_copy(k, h, zk).wait_send()

    def gather_sent():
        for h in range(2):
            all_sent(c_copy, h, rep)
            all_sent(q_copy, h, rep)

    def upper_sent():
        @pl.when(sec == 1)
        def _():
            @pl.loop(0, parts)
            def _(n):
                u_copy(n).wait_send()

    local_start()
    meet()
    gains_start()
    grads_start()
    scales()
    gains_wait()
    norm()
    grads_pass()
    normed_start(0)
    normed_start(1)
    grads_wait()
    normed_wait(0)
    wgrad_other(0)
    wgrad_own(0)
    normed_wait(1)
    weights_start()
    wgrad_other(1)
    plane_start(0)
    wgrad_own(1)
    plane_start(1)
    weights_across()
    back_start(side, yh)
    plane_wait(0)
    plane_sum(0)
    z_start(0)
    plane_wait(1)
    plane_sum(1)
    z_start(1)
    swap_wait(yh)
    back_start(1 - side, yh)
    weights_pass()
    back_start(side, 1 - yh)
    z_wait(0)
    z_sum(0)
    gather_start(0)
    z_wait(1)
    z_sum(1)
    gather_start(1)
    swap_wait(1 - yh)
    back_start(1 - side, 1 - yh)
    back_wait(0)
    dots(0)
    back_wait(1)
    dots(1)
    tcopy.wait()
    owner()
    gather_wait(0)
    gather_wait(1)
    gradients_out()
    gains_sent()
    grads_sent()
    passed_sent()
    weights_sent()
    across_sent()
    swap_sent()
    twin_sent()
    for i in range(2):
        all_sent(x_copy, i, me)
        all_sent(x_copy, 2 + i, me)
        all_sent(a_copy, i, rep)
    back_sent()
    z_sent()
    gather_sent()
    upper_sent()


def local(layer_input, value_grad, value_weight, norm_gain, top_grad):
    reps, groups = lax.axis_size("rep"), lax.axis_size("fsdp")
    _, micro, rows, width = layer_input.shape
    vw = value_grad.shape[3]
    tokens = micro * rows
    bw = value_weight.shape[1]
    blocks = width // bw
    slice_rows = bw // (2 * reps)
    norm_scale = float(tokens * reps * groups) ** (-0.5)
    hbm = pl.BlockSpec(memory_space=pltpu.HBM)
    vmem = pl.BlockSpec(memory_space=pltpu.VMEM)
    dma = pltpu.SemaphoreType.DMA
    grad, wgrad, ggrad = pl.pallas_call(
        functools.partial(kernel, norm_scale),
        out_shape=(
            pltpu.VMEM((tokens, width), BF16),
            pltpu.VMEM((bw, vw), BF16),
            pltpu.VMEM((16, 128), F32),
        ),
        in_specs=[hbm, hbm, hbm, vmem, hbm],
        out_specs=(vmem, vmem, vmem),
        scratch_shapes=[
            pltpu.VMEM((tokens, width), BF16),
            pltpu.VMEM((tokens, width), BF16),
            pltpu.VMEM((bw, vw), BF16),
            pltpu.VMEM((8, bw), F32),
            pltpu.VMEM((blocks, 8, bw), F32),
            pltpu.VMEM((tokens, 128), F32),
            pltpu.VMEM((blocks, 2, tokens, bw // 2), F32),
            pltpu.VMEM((tokens, 128), F32),
            pltpu.VMEM((blocks, 2, tokens, bw // 2), BF16),
            pltpu.VMEM((4, 8 * tokens, bw // 2), BF16),
            pltpu.VMEM((8 * tokens, vw), BF16),
            pltpu.VMEM((2, bw, vw), BF16),
            pltpu.VMEM((2, bw // 2, vw), BF16),
            pltpu.VMEM((2, bw // 2, vw), BF16),
            pltpu.VMEM((2, bw // 2, vw), F32),
            pltpu.VMEM((2, bw // 2, vw), BF16),
            pltpu.VMEM((2, 8, slice_rows, vw), BF16),
            pltpu.VMEM((2, 4, slice_rows, vw), BF16),
            pltpu.VMEM((2, 4, slice_rows, vw), BF16),
            pltpu.VMEM((2, 2, 8 * tokens, bw // 2), BF16),
            pltpu.VMEM((blocks, 2, tokens, bw // 2), BF16),
            pltpu.VMEM((tokens, width), BF16),
            pltpu.VMEM((2, 8, 8, 128), F32),
            dma((6,)),
            dma((16,)), dma((16,)),
            dma((7,)), dma((8,)),
            dma((8, 4)), dma((8, 4)),
            dma((3,)), dma((1,)), dma((1,)), dma((1,)), dma((2,)), dma((2,)),
            dma((2,)), dma((2,)),
            dma((8, 2)), dma((8, 2)),
            dma((4, 2)), dma((4, 2)),
            dma((8, 2)), dma((8, 2)), dma((8, 2)), dma((8, 2)),
            dma((8, 2, 2)), dma((16, 2)),
            dma((4,)), dma((4,)),
        ],
        compiler_params=pltpu.CompilerParams(
            collective_id=0, has_side_effects=True, vmem_limit_bytes=59 * 1024 * 1024
        ),
        name="relay",
    )(
        layer_input.reshape(tokens, width),
        value_grad.reshape(tokens, vw),
        value_weight[0],
        norm_gain,
        top_grad.reshape(tokens, width),
    )
    gain_grad = ggrad[:, :slice_rows].reshape(1, bw) / norm_gain.astype(F32)
    return grad.reshape(layer_input.shape), wgrad.astype(F32)[None], gain_grad


def solution(mesh):
    return jax.shard_map(
        local,
        mesh=mesh,
        in_specs=(
            P("section", None, ("rep", "fsdp"), None),
            P("section", None, ("rep", "fsdp"), None),
            P("section", "fsdp", None),
            P("section", "fsdp"),
            P(None, ("rep", "fsdp"), None),
        ),
        out_specs=(
            P("section", None, ("rep", "fsdp"), None),
            P("section", "fsdp", None),
            P("section", "fsdp"),
        ),
        check_vma=False,
    )
```

```python
import functools

import jax
import jax.numpy as jnp
from jax import lax
from jax.experimental import pallas as pl
from jax.experimental.pallas import tpu as pltpu
from jax.sharding import PartitionSpec as P

NORM_EPS = 1e-05
MESH = pl.DeviceIdType.MESH
CHUNKS = 4
DEPTH = 1
NZ = 8
NY = 4
F32 = jnp.float32
BF16 = jnp.bfloat16


def remote(src, dst, send_sem, recv_sem, device):
    return pltpu.make_async_remote_copy(
        src_ref=src, dst_ref=dst, send_sem=send_sem, recv_sem=recv_sem, device_id=device, device_id_type=MESH
    )


def kernel(
    norm_scale,
    x_hbm, g_hbm, w_hbm, gain_ref, top_hbm,
    ig_ref, wg_ref, gg_ref,
    xbuf, topbuf, wown, gain_src, gain_all, scale_buf, gx, acc_buf, nb, xr, gr, wr, pt, rt, po, pb, ra, sb, rb, db, dr, upper, ggbuf,
    local_sem, gain_ss, gain_rs, g_ss, g_rs, x_ss, x_rs, w_ss, w_rs, w2_ss, w2_rs, w3_ss, w3_rs,
    t_ss, t_rs, a_ss, a_rs, b_ss, b_rs, c_ss, c_rs, q_ss, q_rs, d_ss, d_rs, u_ss, u_rs,
):
    tokens, width = xbuf.shape
    bw, vw = w_hbm.shape
    blocks, hw = width // bw, bw // 2
    chunks, cw, _ = po.shape
    rows = sb.shape[2]
    rep = lax.axis_index("rep")
    fs = lax.axis_index("fsdp")
    sec = lax.axis_index("section")
    xl, y, xh, z = rep % 2, rep // 2, fs // NZ, fs % NZ
    yp = (y + 1 + 2 * ((y + sec) % 2)) % NY
    zp = (z + 1 + (NZ - 2) * ((z + sec) % 2)) % NZ
    jy, jz = y % 2, z % 2
    xb = xh + sec * ((xl + xh) % 2 - xh)
    side = xl + sec * (xh - xl)
    twin = {"rep": y * 2 + 1 - xl, "fsdp": (xh + sec * (1 - 2 * xh)) * NZ + z}
    me = xb * 4 + jy * 2 + jz

    def half_of(label, i):
        return label[0] + sec * (i - label[0])

    def zprime(label, i):
        return label[2] + 2 * ((2 * label[1] + i + sec * ((label[0] + i) % 2 - i + 2)) % 4)

    def member(flip):
        fh, fy, fz = flip // 4, (flip // 2) % 2, flip % 2
        mxl = xl + fh * (1 - 2 * xl)
        mxh = xh + fh * (1 - sec) * (1 - 2 * xh)
        my = y + fy * (yp - y)
        mz = z + fz * (zp - z)
        label = (xb + fh * (1 - 2 * xb), my % 2, mz % 2)
        device = {"rep": my * 2 + mxl, "fsdp": mxh * NZ + mz}
        return device, label, label[0] * 4 + label[1] * 2 + label[2]

    def block(label, i):
        return half_of(label, i) * NZ + zprime(label, i)

    mine = (xb, jy, jz)

    def rows_of(m):
        return pl.ds(pl.multiple_of(m * tokens, tokens), tokens)

    my_rows = rows_of(me)
    other = (me + 4) % 8

    def columns(b):
        return pl.ds(pl.multiple_of(b * bw, bw), bw)

    xcopy = pltpu.make_async_copy(x_hbm, xbuf, local_sem.at[0])
    tcopy = pltpu.make_async_copy(top_hbm, topbuf, local_sem.at[1])
    wcopy = pltpu.make_async_copy(w_hbm, wown, local_sem.at[2])
    gcopy = pltpu.make_async_copy(g_hbm, gr.at[my_rows], local_sem.at[3])

    def local_start():
        for copy in (xcopy, gcopy, wcopy, tcopy):
            copy.start()
        gain_src[...] = jnp.zeros(gain_src.shape, F32)
        ggbuf[rep] = jnp.zeros(ggbuf.shape[1:], F32)
        for k in range(bw // 128):
            gain_src[k : k + 1] = gain_ref[:, k * 128 : (k + 1) * 128].astype(F32)
        gain_all[fs] = gain_src[...]

    def meet():
        barrier = pltpu.get_barrier_semaphore()

        def hello(device):
            pl.semaphore_signal(barrier, inc=1, device_id=device, device_id_type=MESH)

        @pl.loop(1, 8)
        def _(f):
            hello(member(f)[0])
            hello({"rep": (rep + f) % 8})
            hello({"rep": (rep + f) % 8, "fsdp": (1 - xh) * NZ + z})

        @pl.loop(1, 16)
        def _(k):
            hello({"fsdp": (fs + k) % 16})

        hello({"section": 1 - sec})
        pl.semaphore_wait(barrier, 3 * 7 + 15 + 1)

    def gain_copy(k, owner):
        return remote(gain_src, gain_all.at[owner], gain_ss.at[k], gain_rs.at[owner], {"fsdp": (fs + k) % 16})

    def gains_start():
        @pl.loop(1, 16)
        def _(k):
            gain_copy(k, fs).start()

    def gains_wait():
        @pl.loop(1, 16)
        def _(k):
            gain_copy(k, (fs + k) % 16).wait_recv()

    def g_copy(n, f, owner, src):
        return remote(src, gr.at[rows_of(owner)], g_ss.at[n], g_rs.at[owner], member(f)[0])

    def g_pass(n, f, flip):
        owner = member(flip)[2]
        return g_copy(n, f, owner, gr.at[rows_of(owner)])

    def grads_start():
        for n, f in enumerate((2, 1, 4)):
            g_copy(n, f, me, g_hbm).start()

    def grads_over_z():
        g_pass(3, 1, 2).wait_recv()
        g_pass(3, 1, 2).start()
        g_pass(4, 4, 2).start()

    def grads_over_x():
        for n, flip in ((5, 1), (6, 3)):
            g_pass(n, 4, flip).wait_recv()
            g_pass(n, 4, flip).start()

    def grads_wait():
        gcopy.wait()

        @pl.loop(4, 8)
        def _(f):
            g_pass(0, 4, f).wait_recv()

    root = z == zprime(mine, side)
    wh = w_hbm.shape[0] // 2
    yh = y // 2

    def w_part(p):
        return pl.ds(pl.multiple_of(p * wh, wh), wh)

    def w_copy(n):
        return remote(
            w_hbm.at[w_part(yh)], wr.at[side, w_part(yh)], w_ss.at[n], w_rs.at[0],
            {"fsdp": xh * NZ + (z + (2, 6, 4)[n]) % NZ},
        )

    w_local = pltpu.make_async_copy(w_hbm.at[w_part(yh)], wr.at[side, w_part(yh)], local_sem.at[4])

    def w_across(p):
        return remote(
            wr.at[side, w_part(yh)], wr.at[side, w_part(p)], w2_ss.at[0], w2_rs.at[0], {"rep": ((y + 2) % NY) * 2 + xl}
        )

    def w_swap(n, p, owner):
        return remote(
            wr.at[side, w_part(p)], wr.at[owner, w_part(p)], w3_ss.at[n], w3_rs.at[p], twin
        )

    def weights_start():
        @pl.when(root)
        def _():
            w_local.start()
            for n in range(3):
                w_copy(n).start()

    def weights_across():
        @pl.when(root)
        def _():
            w_local.wait()

        @pl.when(jnp.logical_not(root))
        def _():
            w_copy(0).wait_recv()

        w_across(yh).start()
        w_swap(0, yh, side).start()

    def weights_pass():
        w_across(1 - yh).wait_recv()
        w_swap(1, 1 - yh, side).start()

    def swap_wait(p):
        w_swap(0, p, 1 - side).wait_recv()

    def scales():
        xcopy.wait()

        def squares(b, acc):
            v = xbuf[:, columns(b)].astype(F32)
            v = v * v
            for k in range(bw // 128):
                acc = acc + v[:, k * 128 : (k + 1) * 128]
            return acc

        acc = lax.fori_loop(0, blocks, squares, jnp.zeros((tokens, 128), F32))
        scale = lax.rsqrt(jnp.sum(acc, axis=1, keepdims=True) / width + NORM_EPS)
        scale_buf[...] = jnp.broadcast_to(scale, scale_buf.shape)

    def norm():
        @pl.loop(0, blocks)
        def _(b):
            for k in range(bw // 128):
                lanes = slice(k * 128 % hw, k * 128 % hw + 128)
                cols = pl.ds(pl.multiple_of(b * bw + k * 128, 128), 128)
                v = xbuf[:, cols].astype(F32) * scale_buf[...]
                v = v * gain_all[b, k : k + 1, :]
                gx[b, k * 128 // hw, :, lanes] = v
                nb[b, k * 128 // cw, :, k * 128 % cw : k * 128 % cw + 128] = v.astype(BF16)

    def x_copy(f, n, owner):
        device, label, _ = member(f)
        return remote(
            nb.at[block(label, n % 2), n // 2], xr.at[n, rows_of(owner)], x_ss.at[f, n], x_rs.at[owner, n], device
        )

    def normed_start(h):
        for i in range(2):
            n = 2 * h + i

            @pl.loop(1, 8)
            def _(f):
                if h >= DEPTH:
                    x_copy(f, n - 2 * DEPTH, me).wait_send()
                x_copy(f, n, me).start()

            xr[n, my_rows] = nb[block(mine, i), h]

    def normed_wait(h):
        @pl.loop(1, 8)
        def _(f):
            for i in range(2):
                x_copy(f, 2 * h + i, member(f)[2]).wait_recv()

    def partial(n):
        return lax.dot_general(xr[n], gr[...], (((0,), (0,)), ((), ())), preferred_element_type=F32)

    def t_copy(h):
        return remote(pt.at[h], rt.at[h], t_ss.at[h], t_rs.at[h], twin)

    def wgrad_other(h):
        pt[h] = partial(2 * h + 1 - side).astype(BF16)
        t_copy(h).start()

    def wgrad_own(h):
        po[h] = partial(2 * h + side)

    def slice_of(c):
        return pl.ds(pl.multiple_of(c * rows, rows), rows)

    def a_copy(k, h, sender):
        c = (rep + k) % 8
        return remote(pb.at[h, slice_of(c)], ra.at[h, sender], a_ss.at[k, h], a_rs.at[sender, h], {"rep": c})

    def plane_start(h):
        t_copy(h).wait_recv()
        pb[h] = (po[h] + rt[h].astype(F32)).astype(BF16)

        @pl.loop(1, 8)
        def _(k):
            a_copy(k, h, rep).start()

        ra[h, rep] = pb[h, slice_of(rep)]

    def plane_wait(h):
        @pl.loop(1, 8)
        def _(k):
            a_copy(k, h, (rep + k) % 8).wait_recv()

    def plane_sum(h):
        for ky in range(2):
            for t in range(2):
                total = ra[h, 2 * ky + t].astype(F32) + ra[h, 2 * ky + 4 + t].astype(F32)
                sb[h, 2 * ky + t] = total.astype(BF16)

    def twin_sent():
        for h in range(chunks):
            t_copy(h).wait_send()

    zk = z // 2

    def b_copy(k, h, sender):
        slot = (zk + k) % 4
        return remote(
            sb.at[h, (slot + 2 * sec) % 4], rb.at[h, sender], b_ss.at[k, h], b_rs.at[sender, h],
            {"fsdp": xh * NZ + jz + 2 * slot},
        )

    def z_start(h):
        for k in range(1, 4):
            b_copy(k, h, zk).start()
        rb[h, zk] = sb[h, (zk + 2 * sec) % 4]

    def z_wait(h):
        for k in range(1, 4):
            b_copy(k, h, (zk + k) % 4).wait_recv()

    def out_rows(h, c):
        return pl.ds(pl.multiple_of(h * cw + c * rows, rows), rows)

    def z_sum(h):
        if h == 0:
            wcopy.wait()
        total = (rb[h, 0].astype(F32) + rb[h, 1].astype(F32)) + (rb[h, 2].astype(F32) + rb[h, 3].astype(F32))
        total = total * norm_scale
        wg_ref[out_rows(h, rep)] = total.astype(BF16)
        gg = jnp.sum(total * wown[out_rows(h, rep)].astype(F32), axis=1, keepdims=True)
        gg = jnp.broadcast_to(jnp.concatenate([gg] * (128 // rows), axis=0), (128, 128))
        ggbuf[rep, h : h + 1] = gg.T[0:1]

    def c_copy(k, h, owner):
        part = wg_ref.at[out_rows(h, owner)]
        return remote(part, part, c_ss.at[k, h], c_rs.at[owner, h], {"rep": (rep + k) % 8})

    def q_copy(k, owner):
        return remote(ggbuf.at[owner], ggbuf.at[owner], q_ss.at[k], q_rs.at[owner], {"rep": (rep + k) % 8})

    def gather_start(h):
        @pl.loop(1, 8)
        def _(k):
            c_copy(k, h, rep).start()
            if h == chunks - 1:
                q_copy(k, rep).start()

    def gather_wait():
        @pl.loop(1, 8)
        def _(k):
            for h in range(chunks):
                c_copy(k, h, (rep + k) % 8).wait_recv()
            q_copy(k, (rep + k) % 8).wait_recv()
        gg_ref[...] = ggbuf[...]

    def d_copy(f, i, p, b):
        device, _, m = member(f)
        return remote(db.at[i, p, rows_of(m)], dr.at[b, p], d_ss.at[f, i, p], d_rs.at[b, p], device)

    def back_start(i, p):
        back = lax.dot_general(gr[...], wr[i, w_part(p)], (((1,), (1,)), ((), ())), preferred_element_type=F32)
        db[i, p] = back.astype(BF16)
        b = block(mine, i)

        @pl.loop(1, 8)
        def _(f):
            d_copy(f, i, p, b).start()

        dr[b, p] = db[i, p, my_rows]

    def first_half(f):
        return member(f)[0]["rep"] // 4

    def back_wait(n):
        @pl.loop(1, 8)
        def _(f):
            p = (first_half(f) + n) % 2
            for i in range(2):
                d_copy(f, i, p, block(member(f)[1], i)).wait_recv()

    def back_sent():
        @pl.loop(1, 8)
        def _(f):
            for i in range(2):
                for p in range(2):
                    d_copy(f, i, p, 0).wait_send()

    def dots(n):
        def add(f, acc):
            p = (first_half(f) + n) % 2
            for i in range(2):
                b = block(member(f)[1], i)
                v = dr[b, p].astype(F32) * gx[b, p]
                for k in range(hw // 128):
                    acc = acc + v[:, k * 128 : (k + 1) * 128]
            return acc

        start = jnp.zeros((tokens, 128), F32) if n == 0 else acc_buf[...]
        acc = lax.fori_loop(0, 8, add, start)
        if n == 0:
            acc_buf[...] = acc
        else:
            scale = scale_buf[:, 0:1]
            avg = jnp.sum(acc, axis=1, keepdims=True) / width
            acc_buf[...] = jnp.broadcast_to(scale * scale * avg, acc.shape)

    parts = u_ss.shape[0]
    part_rows = tokens // parts

    def part_of(n):
        return pl.ds(pl.multiple_of(n * part_rows, part_rows), part_rows)

    def u_copy(n):
        return remote(ig_ref.at[part_of(n)], upper.at[part_of(n)], u_ss.at[n], u_rs.at[n], {"section": 0})

    def owner():
        def finish(part, top):
            sc = scale_buf[part, :]
            c2 = acc_buf[part, :]

            @pl.loop(0, blocks)
            def _(b):
                for k in range(bw // 128):
                    cols = pl.ds(pl.multiple_of(b * bw + k * 128, 128), 128)
                    half_lanes = slice(k * 128 % hw, k * 128 % hw + 128)
                    v = dr[b, k * 128 // hw, part, half_lanes].astype(F32) * gain_all[b, k : k + 1, :] * sc
                    v = (v - xbuf[part, cols].astype(F32) * c2).astype(BF16)
                    if top:
                        v = (topbuf[part, cols].astype(F32) + v.astype(F32)).astype(BF16)
                    ig_ref[part, cols] = v

        @pl.when(sec == 1)
        def _():
            @pl.loop(0, parts)
            def _(n):
                finish(part_of(n), True)
                u_copy(n).start()

        @pl.when(sec == 0)
        def _():
            @pl.loop(0, parts)
            def _(n):
                finish(part_of(n), False)

            @pl.loop(0, parts)
            def _(n):
                u_copy(n).wait_recv()
                part = part_of(n)
                for k in range(width // 1024):
                    cols = slice(k * 1024, (k + 1) * 1024)
                    v = upper[part, cols].astype(F32) + ig_ref[part, cols].astype(F32)
                    ig_ref[part, cols] = v.astype(BF16)

    def gains_sent():
        @pl.loop(1, 16)
        def _(k):
            gain_copy(k, fs).wait_send()

    def grads_sent():
        for n in range(7):
            g_copy(n, 4, me, g_hbm).wait_send()

    def weights_sent():
        @pl.when(root)
        def _():
            for n in range(3):
                w_copy(n).wait_send()

    def across_sent():
        w_across(yh).wait_send()
        w_swap(0, yh, side).wait_send()

    def swap_sent():
        w_swap(1, 1 - yh, side).wait_send()

    def all_sent(copy, i, owner):
        @pl.loop(1, 8)
        def _(k):
            copy(k, i, owner).wait_send()

    def z_sent():
        for h in range(chunks):
            for k in range(1, 4):
                b_copy(k, h, zk).wait_send()

    def gather_sent():
        for h in range(chunks):
            all_sent(c_copy, h, rep)

        @pl.loop(1, 8)
        def _(k):
            q_copy(k, rep).wait_send()

    def upper_sent():
        @pl.when(sec == 1)
        def _():
            @pl.loop(0, parts)
            def _(n):
                u_copy(n).wait_send()

    local_start()
    meet()
    gains_start()
    grads_start()
    scales()
    grads_over_z()
    gains_wait()
    norm()
    normed_start(0)
    normed_start(1)
    grads_over_x()
    normed_start(2)
    weights_start()
    grads_wait()
    normed_wait(0)
    wgrad_other(0)
    normed_start(3)
    wgrad_own(0)
    normed_wait(1)
    wgrad_other(1)
    plane_start(0)
    wgrad_own(1)
    normed_wait(2)
    wgrad_other(2)
    plane_start(1)
    weights_across()
    wgrad_own(2)
    plane_wait(0)
    plane_sum(0)
    z_start(0)
    normed_wait(3)
    wgrad_other(3)
    plane_start(2)
    wgrad_own(3)
    plane_wait(1)
    plane_sum(1)
    z_start(1)
    plane_start(3)
    weights_pass()
    z_wait(0)
    z_sum(0)
    gather_start(0)
    back_start(side, yh)
    plane_wait(2)
    plane_sum(2)
    z_start(2)
    z_wait(1)
    z_sum(1)
    gather_start(1)
    plane_wait(3)
    plane_sum(3)
    z_start(3)
    swap_wait(yh)
    back_start(1 - side, yh)
    z_wait(2)
    z_sum(2)
    gather_start(2)
    back_start(side, 1 - yh)
    z_wait(3)
    z_sum(3)
    gather_start(3)
    swap_wait(1 - yh)
    back_start(1 - side, 1 - yh)
    back_wait(0)
    dots(0)
    back_wait(1)
    dots(1)
    tcopy.wait()
    owner()
    gather_wait()
    gains_sent()
    grads_sent()
    weights_sent()
    across_sent()
    swap_sent()
    twin_sent()
    for h in range(chunks):
        all_sent(a_copy, h, rep)
        if h >= chunks - DEPTH:
            all_sent(x_copy, 2 * h, me)
            all_sent(x_copy, 2 * h + 1, me)
    back_sent()
    z_sent()
    gather_sent()
    upper_sent()


def local(layer_input, value_grad, value_weight, norm_gain, top_grad):
    reps, groups = lax.axis_size("rep"), lax.axis_size("fsdp")
    _, micro, rows, width = layer_input.shape
    vw = value_grad.shape[3]
    tokens = micro * rows
    bw = value_weight.shape[1]
    blocks = width // bw
    cw = bw // CHUNKS
    slice_rows = cw // reps
    norm_scale = float(tokens * reps * groups) ** (-0.5)
    hbm = pl.BlockSpec(memory_space=pltpu.HBM)
    vmem = pl.BlockSpec(memory_space=pltpu.VMEM)
    dma = pltpu.SemaphoreType.DMA
    grad, wgrad, ggrad = pl.pallas_call(
        functools.partial(kernel, norm_scale),
        out_shape=(
            pltpu.VMEM((tokens, width), BF16),
            pltpu.VMEM((bw, vw), BF16),
            pltpu.VMEM((8, 8, 128), F32),
        ),
        in_specs=[hbm, hbm, hbm, vmem, hbm],
        out_specs=(vmem, vmem, vmem),
        scratch_shapes=[
            pltpu.VMEM((tokens, width), BF16),
            pltpu.VMEM((tokens, width), BF16),
            pltpu.VMEM((bw, vw), BF16),
            pltpu.VMEM((8, 128), F32),
            pltpu.VMEM((blocks, 8, 128), F32),
            pltpu.VMEM((tokens, 128), F32),
            pltpu.VMEM((blocks, 2, tokens, bw // 2), F32),
            pltpu.VMEM((tokens, 128), F32),
            pltpu.VMEM((blocks, CHUNKS, tokens, cw), BF16),
            pltpu.VMEM((2 * CHUNKS, 8 * tokens, cw), BF16),
            pltpu.VMEM((8 * tokens, vw), BF16),
            pltpu.VMEM((2, bw, vw), BF16),
            pltpu.VMEM((CHUNKS, cw, vw), BF16),
            pltpu.VMEM((CHUNKS, cw, vw), BF16),
            pltpu.VMEM((CHUNKS, cw, vw), F32),
            pltpu.VMEM((CHUNKS, cw, vw), BF16),
            pltpu.VMEM((CHUNKS, 8, slice_rows, vw), BF16),
            pltpu.VMEM((CHUNKS, 4, slice_rows, vw), BF16),
            pltpu.VMEM((CHUNKS, 4, slice_rows, vw), BF16),
            pltpu.VMEM((2, 2, 8 * tokens, bw // 2), BF16),
            pltpu.VMEM((blocks, 2, tokens, bw // 2), BF16),
            pltpu.VMEM((tokens, width), BF16),
            pltpu.VMEM((8, 8, 128), F32),
            dma((6,)),
            dma((16,)), dma((16,)),
            dma((7,)), dma((8,)),
            dma((8, 2 * CHUNKS)), dma((8, 2 * CHUNKS)),
            dma((3,)), dma((1,)), dma((1,)), dma((1,)), dma((2,)), dma((2,)),
            dma((CHUNKS,)), dma((CHUNKS,)),
            dma((8, CHUNKS)), dma((8, CHUNKS)),
            dma((4, CHUNKS)), dma((4, CHUNKS)),
            dma((8, CHUNKS)), dma((8, CHUNKS)), dma((8,)), dma((8,)),
            dma((8, 2, 2)), dma((16, 2)),
            dma((4,)), dma((4,)),
        ],
        compiler_params=pltpu.CompilerParams(
            collective_id=0, has_side_effects=True, vmem_limit_bytes=59 * 1024 * 1024
        ),
        name="relay",
    )(
        layer_input.reshape(tokens, width),
        value_grad.reshape(tokens, vw),
        value_weight[0],
        norm_gain,
        top_grad.reshape(tokens, width),
    )
    gain_grad = ggrad[:, :CHUNKS, :slice_rows].swapaxes(0, 1).reshape(1, bw) / norm_gain.astype(F32)
    return grad.reshape(layer_input.shape), wgrad.astype(F32)[None], gain_grad


def solution(mesh):
    return jax.shard_map(
        local,
        mesh=mesh,
        in_specs=(
            P("section", None, ("rep", "fsdp"), None),
            P("section", None, ("rep", "fsdp"), None),
            P("section", "fsdp", None),
            P("section", "fsdp"),
            P(None, ("rep", "fsdp"), None),
        ),
        out_specs=(
            P("section", None, ("rep", "fsdp"), None),
            P("section", "fsdp", None),
            P("section", "fsdp"),
        ),
        check_vma=False,
    )
```

```python
import functools

import jax
import jax.numpy as jnp
from jax import lax
from jax.experimental import pallas as pl
from jax.experimental.pallas import tpu as pltpu
from jax.sharding import PartitionSpec as P

NORM_EPS = 1e-05
MESH = pl.DeviceIdType.MESH
CHUNKS = 4
DEPTH = 1
NZ = 8
NY = 4
F32 = jnp.float32
BF16 = jnp.bfloat16


def remote(src, dst, send_sem, recv_sem, device):
    return pltpu.make_async_remote_copy(
        src_ref=src, dst_ref=dst, send_sem=send_sem, recv_sem=recv_sem, device_id=device, device_id_type=MESH
    )


def kernel(
    norm_scale,
    x_hbm, g_hbm, w_hbm, gain_ref, top_hbm,
    ig_ref, wg_ref, gg_ref,
    xbuf, topbuf, wown, gain_src, gain_all, scale_buf, gx, acc_buf, nb, xr, gr, wr, pt, rt, po, pb, ra, sb, rb, db, dr, upper, ggbuf,
    local_sem, gain_ss, gain_rs, g_ss, g_rs, x_ss, x_rs, w_ss, w_rs, w2_ss, w2_rs, w3_ss, w3_rs,
    t_ss, t_rs, a_ss, a_rs, b_ss, b_rs, c_ss, c_rs, q_ss, q_rs, d_ss, d_rs, u_ss, u_rs,
):
    tokens, width = xbuf.shape
    bw, vw = w_hbm.shape
    blocks, hw = width // bw, bw // 2
    chunks, cw, _ = po.shape
    rows = sb.shape[2]
    rep = lax.axis_index("rep")
    fs = lax.axis_index("fsdp")
    sec = lax.axis_index("section")
    xl, y, xh, z = rep % 2, rep // 2, fs // NZ, fs % NZ
    yp = (y + 1 + 2 * ((y + sec) % 2)) % NY
    zp = (z + 1 + (NZ - 2) * ((z + sec) % 2)) % NZ
    jy, jz = y % 2, z % 2
    xb = xh + sec * ((xl + xh) % 2 - xh)
    side = xl + sec * (xh - xl)
    twin = {"rep": y * 2 + 1 - xl, "fsdp": (xh + sec * (1 - 2 * xh)) * NZ + z}
    me = xb * 4 + jy * 2 + jz

    def half_of(label, i):
        return label[0] + sec * (i - label[0])

    def zprime(label, i):
        return label[2] + 2 * ((2 * label[1] + i + sec * ((label[0] + i) % 2 - i + 2)) % 4)

    def member(flip):
        fh, fy, fz = flip // 4, (flip // 2) % 2, flip % 2
        mxl = xl + fh * (1 - 2 * xl)
        mxh = xh + fh * (1 - sec) * (1 - 2 * xh)
        my = y + fy * (yp - y)
        mz = z + fz * (zp - z)
        label = (xb + fh * (1 - 2 * xb), my % 2, mz % 2)
        device = {"rep": my * 2 + mxl, "fsdp": mxh * NZ + mz}
        return device, label, label[0] * 4 + label[1] * 2 + label[2]

    def block(label, i):
        return half_of(label, i) * NZ + zprime(label, i)

    mine = (xb, jy, jz)

    def rows_of(m):
        return pl.ds(pl.multiple_of(m * tokens, tokens), tokens)

    my_rows = rows_of(me)
    other = (me + 4) % 8

    def columns(b):
        return pl.ds(pl.multiple_of(b * bw, bw), bw)

    xcopy = pltpu.make_async_copy(x_hbm, xbuf, local_sem.at[0])
    tcopy = pltpu.make_async_copy(top_hbm, topbuf, local_sem.at[1])
    wcopy = pltpu.make_async_copy(w_hbm, wown, local_sem.at[2])
    gcopy = pltpu.make_async_copy(g_hbm, gr.at[my_rows], local_sem.at[3])

    def local_start():
        for copy in (xcopy, gcopy, wcopy, tcopy):
            copy.start()
        gain_src[...] = jnp.zeros(gain_src.shape, F32)
        ggbuf[rep] = jnp.zeros(ggbuf.shape[1:], F32)
        for k in range(bw // 128):
            gain_src[k : k + 1] = gain_ref[:, k * 128 : (k + 1) * 128].astype(F32)
        gain_all[fs] = gain_src[...]

    def meet():
        barrier = pltpu.get_barrier_semaphore()

        def hello(device):
            pl.semaphore_signal(barrier, inc=1, device_id=device, device_id_type=MESH)

        @pl.loop(1, 8)
        def _(f):
            hello(member(f)[0])
            hello({"rep": (rep + f) % 8})
            hello({"rep": (rep + f) % 8, "fsdp": (1 - xh) * NZ + z})

        @pl.loop(1, 16)
        def _(k):
            hello({"fsdp": (fs + k) % 16})

        hello({"section": 1 - sec})
        pl.semaphore_wait(barrier, 3 * 7 + 15 + 1)

    def gain_copy(k, owner):
        return remote(gain_src, gain_all.at[owner], gain_ss.at[k], gain_rs.at[owner], {"fsdp": (fs + k) % 16})

    def gains_start():
        @pl.loop(1, 16)
        def _(k):
            gain_copy(k, fs).start()

    def gains_wait():
        @pl.loop(1, 16)
        def _(k):
            gain_copy(k, (fs + k) % 16).wait_recv()

    def g_copy(n, f, owner, src):
        return remote(src, gr.at[rows_of(owner)], g_ss.at[n], g_rs.at[owner], member(f)[0])

    def g_pass(n, f, flip):
        owner = member(flip)[2]
        return g_copy(n, f, owner, gr.at[rows_of(owner)])

    def grads_start():
        gcopy.wait()
        for n, f in enumerate((2, 1, 4)):
            g_copy(n, f, me, gr.at[my_rows]).start()

    def grads_over_z():
        g_pass(3, 1, 2).wait_recv()
        g_pass(3, 1, 2).start()
        g_pass(4, 4, 2).start()

    def grads_over_x():
        for n, flip in ((5, 1), (6, 3)):
            g_pass(n, 4, flip).wait_recv()
            g_pass(n, 4, flip).start()

    def grads_wait():
        @pl.loop(4, 8)
        def _(f):
            g_pass(0, 4, f).wait_recv()

    root = z == zprime(mine, side)
    wh = w_hbm.shape[0] // 2
    yh = y // 2

    def w_part(p):
        return pl.ds(pl.multiple_of(p * wh, wh), wh)

    def w_copy(n):
        return remote(
            wown.at[w_part(yh)], wr.at[side, w_part(yh)], w_ss.at[n], w_rs.at[0],
            {"fsdp": xh * NZ + (z + (2, 6, 4)[n]) % NZ},
        )

    w_local = pltpu.make_async_copy(w_hbm.at[w_part(yh)], wr.at[side, w_part(yh)], local_sem.at[4])

    def w_across(p):
        return remote(
            wr.at[side, w_part(yh)], wr.at[side, w_part(p)], w2_ss.at[0], w2_rs.at[0], {"rep": ((y + 2) % NY) * 2 + xl}
        )

    def w_swap(n, p, owner):
        return remote(
            wr.at[side, w_part(p)], wr.at[owner, w_part(p)], w3_ss.at[n], w3_rs.at[p], twin
        )

    def weights_start():
        wcopy.wait()

        @pl.when(root)
        def _():
            w_local.start()
            for n in range(3):
                w_copy(n).start()

    def weights_across():
        @pl.when(root)
        def _():
            w_local.wait()

        @pl.when(jnp.logical_not(root))
        def _():
            w_copy(0).wait_recv()

        w_across(yh).start()
        w_swap(0, yh, side).start()

    def weights_pass():
        w_across(1 - yh).wait_recv()
        w_swap(1, 1 - yh, side).start()

    def swap_wait(p):
        w_swap(0, p, 1 - side).wait_recv()

    def scales():
        xcopy.wait()

        def squares(b, acc):
            v = xbuf[:, columns(b)].astype(F32)
            v = v * v
            for k in range(bw // 128):
                acc = acc + v[:, k * 128 : (k + 1) * 128]
            return acc

        acc = lax.fori_loop(0, blocks, squares, jnp.zeros((tokens, 128), F32))
        scale = lax.rsqrt(jnp.sum(acc, axis=1, keepdims=True) / width + NORM_EPS)
        scale_buf[...] = jnp.broadcast_to(scale, scale_buf.shape)

    def norm():
        @pl.loop(0, blocks)
        def _(b):
            for k in range(bw // 128):
                lanes = slice(k * 128 % hw, k * 128 % hw + 128)
                cols = pl.ds(pl.multiple_of(b * bw + k * 128, 128), 128)
                v = xbuf[:, cols].astype(F32) * scale_buf[...]
                v = v * gain_all[b, k : k + 1, :]
                gx[b, k * 128 // hw, :, lanes] = v
                nb[b, k * 128 // cw, :, k * 128 % cw : k * 128 % cw + 128] = v.astype(BF16)

    def x_copy(f, n, owner):
        device, label, _ = member(f)
        return remote(
            nb.at[block(label, n % 2), n // 2], xr.at[n, rows_of(owner)], x_ss.at[f, n], x_rs.at[owner, n], device
        )

    def normed_start(h):
        for i in range(2):
            n = 2 * h + i

            @pl.loop(1, 8)
            def _(f):
                if h >= DEPTH:
                    x_copy(8 - f, n - 2 * DEPTH, me).wait_send()
                x_copy(8 - f, n, me).start()

            xr[n, my_rows] = nb[block(mine, i), h]

    def normed_wait(h):
        @pl.loop(1, 8)
        def _(f):
            for i in range(2):
                x_copy(f, 2 * h + i, member(f)[2]).wait_recv()

    def partial(n):
        return lax.dot_general(xr[n], gr[...], (((0,), (0,)), ((), ())), preferred_element_type=F32)

    def t_copy(h):
        return remote(pt.at[h], rt.at[h], t_ss.at[h], t_rs.at[h], twin)

    def wgrad_other(h):
        pt[h] = partial(2 * h + 1 - side).astype(BF16)
        t_copy(h).start()

    def wgrad_own(h):
        po[h] = partial(2 * h + side)

    def slice_of(c):
        return pl.ds(pl.multiple_of(c * rows, rows), rows)

    def a_copy(k, h, sender):
        c = (rep + k) % 8
        return remote(pb.at[h, slice_of(c)], ra.at[h, sender], a_ss.at[k, h], a_rs.at[sender, h], {"rep": c})

    def plane_start(h):
        t_copy(h).wait_recv()
        pb[h] = (po[h] + rt[h].astype(F32)).astype(BF16)

        @pl.loop(1, 8)
        def _(k):
            a_copy(k, h, rep).start()

        ra[h, rep] = pb[h, slice_of(rep)]

    def plane_wait(h):
        @pl.loop(1, 8)
        def _(k):
            a_copy(k, h, (rep + k) % 8).wait_recv()

    def plane_sum(h):
        for ky in range(2):
            for t in range(2):
                total = ra[h, 2 * ky + t].astype(F32) + ra[h, 2 * ky + 4 + t].astype(F32)
                sb[h, 2 * ky + t] = total.astype(BF16)

    def twin_sent():
        for h in range(chunks):
            t_copy(h).wait_send()

    zk = z // 2

    def b_copy(k, h, sender):
        slot = (zk + k) % 4
        return remote(
            sb.at[h, (slot + 2 * sec) % 4], rb.at[h, sender], b_ss.at[k, h], b_rs.at[sender, h],
            {"fsdp": xh * NZ + jz + 2 * slot},
        )

    def z_start(h):
        for k in range(1, 4):
            b_copy(k, h, zk).start()
        rb[h, zk] = sb[h, (zk + 2 * sec) % 4]

    def z_wait(h):
        for k in range(1, 4):
            b_copy(k, h, (zk + k) % 4).wait_recv()

    def out_rows(h, c):
        return pl.ds(pl.multiple_of(h * cw + c * rows, rows), rows)

    def z_sum(h):
        total = (rb[h, 0].astype(F32) + rb[h, 1].astype(F32)) + (rb[h, 2].astype(F32) + rb[h, 3].astype(F32))
        total = total * norm_scale
        wg_ref[out_rows(h, rep)] = total.astype(BF16)
        gg = jnp.sum(total * wown[out_rows(h, rep)].astype(F32), axis=1, keepdims=True)
        gg = jnp.broadcast_to(jnp.concatenate([gg] * (128 // rows), axis=0), (128, 128))
        ggbuf[rep, h : h + 1] = gg.T[0:1]

    def c_copy(k, h, owner):
        part = wg_ref.at[out_rows(h, owner)]
        return remote(part, part, c_ss.at[k, h], c_rs.at[owner, h], {"rep": (rep + k) % 8})

    def q_copy(k, owner):
        return remote(ggbuf.at[owner], ggbuf.at[owner], q_ss.at[k], q_rs.at[owner], {"rep": (rep + k) % 8})

    def gather_start(h):
        @pl.loop(1, 8)
        def _(k):
            c_copy(k, h, rep).start()
            if h == chunks - 1:
                q_copy(k, rep).start()

    def gather_wait():
        @pl.loop(1, 8)
        def _(k):
            for h in range(chunks):
                c_copy(k, h, (rep + k) % 8).wait_recv()
            q_copy(k, (rep + k) % 8).wait_recv()
        gg_ref[...] = ggbuf[...]

    def d_copy(f, i, p, b):
        device, _, m = member(f)
        return remote(db.at[i, p, rows_of(m)], dr.at[b, p], d_ss.at[f, i, p], d_rs.at[b, p], device)

    def back_start(i, p):
        back = lax.dot_general(gr[...], wr[i, w_part(p)], (((1,), (1,)), ((), ())), preferred_element_type=F32)
        db[i, p] = back.astype(BF16)
        b = block(mine, i)

        @pl.loop(1, 8)
        def _(f):
            d_copy(8 - f, i, p, b).start()

        dr[b, p] = db[i, p, my_rows]

    def first_half(f):
        return member(f)[0]["rep"] // 4

    def back_wait(n):
        @pl.loop(1, 8)
        def _(f):
            p = (first_half(f) + n) % 2
            for i in range(2):
                d_copy(f, i, p, block(member(f)[1], i)).wait_recv()

    def back_sent():
        @pl.loop(1, 8)
        def _(f):
            for i in range(2):
                for p in range(2):
                    d_copy(f, i, p, 0).wait_send()

    def dots(n):
        def add(f, acc):
            p = (first_half(f) + n) % 2
            for i in range(2):
                b = block(member(f)[1], i)
                v = dr[b, p].astype(F32) * gx[b, p]
                for k in range(hw // 128):
                    acc = acc + v[:, k * 128 : (k + 1) * 128]
            return acc

        start = jnp.zeros((tokens, 128), F32) if n == 0 else acc_buf[...]
        acc = lax.fori_loop(0, 8, add, start)
        if n == 0:
            acc_buf[...] = acc
        else:
            scale = scale_buf[:, 0:1]
            avg = jnp.sum(acc, axis=1, keepdims=True) / width
            acc_buf[...] = jnp.broadcast_to(scale * scale * avg, acc.shape)

    parts = u_ss.shape[0]
    part_rows = tokens // parts

    def part_of(n):
        return pl.ds(pl.multiple_of(n * part_rows, part_rows), part_rows)

    def u_copy(n):
        return remote(ig_ref.at[part_of(n)], upper.at[part_of(n)], u_ss.at[n], u_rs.at[n], {"section": 0})

    def owner():
        def finish(part, top):
            sc = scale_buf[part, :]
            c2 = acc_buf[part, :]

            @pl.loop(0, blocks)
            def _(b):
                for k in range(bw // 128):
                    cols = pl.ds(pl.multiple_of(b * bw + k * 128, 128), 128)
                    half_lanes = slice(k * 128 % hw, k * 128 % hw + 128)
                    v = dr[b, k * 128 // hw, part, half_lanes].astype(F32) * gain_all[b, k : k + 1, :] * sc
                    v = (v - xbuf[part, cols].astype(F32) * c2).astype(BF16)
                    if top:
                        v = (topbuf[part, cols].astype(F32) + v.astype(F32)).astype(BF16)
                    ig_ref[part, cols] = v

        @pl.when(sec == 1)
        def _():
            @pl.loop(0, parts)
            def _(n):
                finish(part_of(n), True)
                u_copy(n).start()

        @pl.when(sec == 0)
        def _():
            @pl.loop(0, parts)
            def _(n):
                finish(part_of(n), False)

            @pl.loop(0, parts)
            def _(n):
                u_copy(n).wait_recv()
                part = part_of(n)
                for k in range(width // 1024):
                    cols = slice(k * 1024, (k + 1) * 1024)
                    v = upper[part, cols].astype(F32) + ig_ref[part, cols].astype(F32)
                    ig_ref[part, cols] = v.astype(BF16)

    def gains_sent():
        @pl.loop(1, 16)
        def _(k):
            gain_copy(k, fs).wait_send()

    def grads_sent():
        for n in range(7):
            g_copy(n, 4, me, g_hbm).wait_send()

    def weights_sent():
        @pl.when(root)
        def _():
            for n in range(3):
                w_copy(n).wait_send()

    def across_sent():
        w_across(yh).wait_send()
        w_swap(0, yh, side).wait_send()

    def swap_sent():
        w_swap(1, 1 - yh, side).wait_send()

    def all_sent(copy, i, owner):
        @pl.loop(1, 8)
        def _(k):
            copy(k, i, owner).wait_send()

    def z_sent():
        for h in range(chunks):
            for k in range(1, 4):
                b_copy(k, h, zk).wait_send()

    def gather_sent():
        for h in range(chunks):
            all_sent(c_copy, h, rep)

        @pl.loop(1, 8)
        def _(k):
            q_copy(k, rep).wait_send()

    def upper_sent():
        @pl.when(sec == 1)
        def _():
            @pl.loop(0, parts)
            def _(n):
                u_copy(n).wait_send()

    local_start()
    meet()
    gains_start()
    grads_start()
    scales()
    grads_over_z()
    gains_wait()
    norm()
    normed_start(0)
    normed_start(1)
    grads_over_x()
    normed_start(2)
    weights_start()
    grads_wait()
    normed_wait(0)
    wgrad_other(0)
    normed_start(3)
    wgrad_own(0)
    normed_wait(1)
    wgrad_other(1)
    plane_start(0)
    wgrad_own(1)
    normed_wait(2)
    wgrad_other(2)
    plane_start(1)
    weights_across()
    wgrad_own(2)
    plane_wait(0)
    plane_sum(0)
    z_start(0)
    normed_wait(3)
    wgrad_other(3)
    plane_start(2)
    wgrad_own(3)
    plane_wait(1)
    plane_sum(1)
    z_start(1)
    plane_start(3)
    weights_pass()
    z_wait(0)
    z_sum(0)
    gather_start(0)
    back_start(side, yh)
    plane_wait(2)
    plane_sum(2)
    z_start(2)
    z_wait(1)
    z_sum(1)
    gather_start(1)
    plane_wait(3)
    plane_sum(3)
    z_start(3)
    swap_wait(yh)
    back_start(1 - side, yh)
    z_wait(2)
    z_sum(2)
    gather_start(2)
    back_start(side, 1 - yh)
    z_wait(3)
    z_sum(3)
    gather_start(3)
    swap_wait(1 - yh)
    back_start(1 - side, 1 - yh)
    back_wait(0)
    dots(0)
    back_wait(1)
    dots(1)
    tcopy.wait()
    owner()
    gather_wait()
    gains_sent()
    grads_sent()
    weights_sent()
    across_sent()
    swap_sent()
    twin_sent()
    for h in range(chunks):
        all_sent(a_copy, h, rep)
        if h >= chunks - DEPTH:
            all_sent(x_copy, 2 * h, me)
            all_sent(x_copy, 2 * h + 1, me)
    back_sent()
    z_sent()
    gather_sent()
    upper_sent()


def local(layer_input, value_grad, value_weight, norm_gain, top_grad):
    reps, groups = lax.axis_size("rep"), lax.axis_size("fsdp")
    _, micro, rows, width = layer_input.shape
    vw = value_grad.shape[3]
    tokens = micro * rows
    bw = value_weight.shape[1]
    blocks = width // bw
    cw = bw // CHUNKS
    slice_rows = cw // reps
    norm_scale = float(tokens * reps * groups) ** (-0.5)
    hbm = pl.BlockSpec(memory_space=pltpu.HBM)
    vmem = pl.BlockSpec(memory_space=pltpu.VMEM)
    dma = pltpu.SemaphoreType.DMA
    grad, wgrad, ggrad = pl.pallas_call(
        functools.partial(kernel, norm_scale),
        out_shape=(
            pltpu.VMEM((tokens, width), BF16),
            pltpu.VMEM((bw, vw), BF16),
            pltpu.VMEM((8, 8, 128), F32),
        ),
        in_specs=[hbm, hbm, hbm, vmem, hbm],
        out_specs=(vmem, vmem, vmem),
        scratch_shapes=[
            pltpu.VMEM((tokens, width), BF16),
            pltpu.VMEM((tokens, width), BF16),
            pltpu.VMEM((bw, vw), BF16),
            pltpu.VMEM((8, 128), F32),
            pltpu.VMEM((blocks, 8, 128), F32),
            pltpu.VMEM((tokens, 128), F32),
            pltpu.VMEM((blocks, 2, tokens, bw // 2), F32),
            pltpu.VMEM((tokens, 128), F32),
            pltpu.VMEM((blocks, CHUNKS, tokens, cw), BF16),
            pltpu.VMEM((2 * CHUNKS, 8 * tokens, cw), BF16),
            pltpu.VMEM((8 * tokens, vw), BF16),
            pltpu.VMEM((2, bw, vw), BF16),
            pltpu.VMEM((CHUNKS, cw, vw), BF16),
            pltpu.VMEM((CHUNKS, cw, vw), BF16),
            pltpu.VMEM((CHUNKS, cw, vw), F32),
            pltpu.VMEM((CHUNKS, cw, vw), BF16),
            pltpu.VMEM((CHUNKS, 8, slice_rows, vw), BF16),
            pltpu.VMEM((CHUNKS, 4, slice_rows, vw), BF16),
            pltpu.VMEM((CHUNKS, 4, slice_rows, vw), BF16),
            pltpu.VMEM((2, 2, 8 * tokens, bw // 2), BF16),
            pltpu.VMEM((blocks, 2, tokens, bw // 2), BF16),
            pltpu.VMEM((tokens, width), BF16),
            pltpu.VMEM((8, 8, 128), F32),
            dma((6,)),
            dma((16,)), dma((16,)),
            dma((7,)), dma((8,)),
            dma((8, 2 * CHUNKS)), dma((8, 2 * CHUNKS)),
            dma((3,)), dma((1,)), dma((1,)), dma((1,)), dma((2,)), dma((2,)),
            dma((CHUNKS,)), dma((CHUNKS,)),
            dma((8, CHUNKS)), dma((8, CHUNKS)),
            dma((4, CHUNKS)), dma((4, CHUNKS)),
            dma((8, CHUNKS)), dma((8, CHUNKS)), dma((8,)), dma((8,)),
            dma((8, 2, 2)), dma((16, 2)),
            dma((4,)), dma((4,)),
        ],
        compiler_params=pltpu.CompilerParams(
            collective_id=0, has_side_effects=True, vmem_limit_bytes=59 * 1024 * 1024
        ),
        name="relay",
    )(
        layer_input.reshape(tokens, width),
        value_grad.reshape(tokens, vw),
        value_weight[0],
        norm_gain,
        top_grad.reshape(tokens, width),
    )
    gain_grad = ggrad[:, :CHUNKS, :slice_rows].swapaxes(0, 1).reshape(1, bw) / norm_gain.astype(F32)
    return grad.reshape(layer_input.shape), wgrad.astype(F32)[None], gain_grad


def solution(mesh):
    return jax.shard_map(
        local,
        mesh=mesh,
        in_specs=(
            P("section", None, ("rep", "fsdp"), None),
            P("section", None, ("rep", "fsdp"), None),
            P("section", "fsdp", None),
            P("section", "fsdp"),
            P(None, ("rep", "fsdp"), None),
        ),
        out_specs=(
            P("section", None, ("rep", "fsdp"), None),
            P("section", "fsdp", None),
            P("section", "fsdp"),
        ),
        check_vma=False,
    )
```
